128 devices in a mesh: pix: 32 (over x, z, core), lay: 4 (over y).
Axes of the slice: x: 4, y: 4, z: 4, core: 2. Of those that a mesh axis runs over, the one named last changes fastest.
Arguments:
- pixel_stack: float32 [524288, 512], P('pix', 'lay'), may hold values from -4000 to 4000, as said below
Outputs:
- scores: float32 [524288, 512], P(('pix', 'lay'))
- log_scale: float32 [512], P('lay')
The draws below stay inside these ranges and needn't reach their ends.
Inputs may be any that keep to these rules, and one draw needn't show every extreme that they name: pixel_stack is finite.
All inputs are finite; a program needn't handle non-finite values.
Results may differ from the reference program's by a relative error of at most 0.00013.
Values sent between devices are 32-bit elements; how exact they have to be, the bound alone decides.
No kernel may reach another device: no remote copies, remote signals or barrier semaphores. Data moves between devices by JAX's collectives and lax.ppermute only.
A program may use at most 128 MiB of HBM per device.

```python
import math
import jax
import jax.numpy as jnp
from jax import lax

L = 512
PIXELS = 524288


def draw_pixel_stack(key, part):
    keys = jax.random.split(key, 4)
    position = jnp.arange(PIXELS, dtype=jnp.float32) / PIXELS
    ramp = jnp.exp(position * math.log(3.0))
    row_noise = jnp.exp(jax.random.uniform(keys[0], (PIXELS,), jnp.float32, 0.0, math.log(10.0)))
    col_scale = jnp.exp(jax.random.uniform(keys[1], (L,), jnp.float32, 0.0, math.log(10.0)))
    offset = 2.0 * jax.random.normal(keys[2], (L,), jnp.float32)
    values = jax.random.normal(keys[3], (PIXELS, L), jnp.float32)
    values = jnp.clip(values, -6.0, 6.0)
    return offset + col_scale * (ramp * row_noise)[:, None] * values


def setup_inputs(seed: int = 0) -> dict:
    streams_of = jax.random.split(jax.random.key(seed), 2)
    return {
        "pixel_stack": draw_pixel_stack(jax.random.fold_in(streams_of[1], 71), 0),
    }


def reference(pixel_stack):
    mean = lax.optimization_barrier(jnp.sum(pixel_stack, axis=0)) / PIXELS
    centered = pixel_stack - mean
    spread = lax.optimization_barrier(jnp.sum(centered * centered, axis=0)) / PIXELS
    log_scale = 0.5 * jnp.log(spread + 1e-05)
    standard = centered * lax.rsqrt(spread + 1e-05)
    gram = jnp.dot(standard.T.astype(jnp.float32), standard.astype(jnp.float32), precision=lax.Precision.HIGHEST, preferred_element_type=jnp.float32)
    lower = jnp.linalg.cholesky(gram)
    inverse = lax.linalg.triangular_solve(lower, jnp.eye(L, dtype=gram.dtype), left_side=True, lower=True)
    scores = jnp.dot(standard.astype(jnp.float32), inverse.T.astype(jnp.float32), precision=lax.Precision.HIGHEST, preferred_element_type=jnp.float32)
    return (scores * math.sqrt(PIXELS), log_scale)
```

```python
import functools

import jax
import jax.numpy as jnp
from jax import lax
from jax.experimental import pallas as pl
from jax.experimental.pallas import tpu as pltpu
from jax.sharding import Mesh
from jax.sharding import PartitionSpec as P

EXACT = lax.Precision.HIGHEST
LANES = 128
CHUNKS = 2
TILE = 512
VMEM_LIMIT = 48 * 2**20


def dot(a, b, contract, precision=None):
    return lax.dot_general(
        a, b, (contract, ((), ())), precision=precision, preferred_element_type=jnp.float32
    )


def gram_kernel(last, first, place, own, near, far, back, mean, *rest):
    rest = list(rest)
    held = None if first else rest.pop(0)
    if not first:
        rest.pop(0), rest.pop(0)
    high, low, sums = rest[:3]
    packed = rest[3] if last else None
    step = pl.program_id(0)

    @pl.when(step == 0)
    def _():
        sums[...] = jnp.zeros_like(sums) if first else held[...]

    for away, ref in enumerate((own, near, far, back)):
        layer = lax.rem(place[0] - away + 4, 4)
        lanes = pl.ds(pl.multiple_of(layer * LANES, LANES), LANES)
        value = ref[...].reshape(-1, LANES) - mean[0:1, lanes]
        top = value.astype(jnp.bfloat16)
        high[:, lanes] = top
        low[:, lanes] = (value - top.astype(jnp.float32)).astype(jnp.bfloat16)

    rows = ((0,), (0,))
    half = 2 * LANES
    a, b = high[:, :half], high[:, half:]
    al, bl = low[:, :half], low[:, half:]
    sums[0] += dot(a, a, rows)
    sums[1] += dot(b, b, rows)
    sums[2] += dot(b, a, rows) + dot(b, al, rows) + dot(bl, a, rows)
    sums[3] += dot(a, al, rows)
    sums[4] += dot(b, bl, rows)

    if last:

        @pl.when(step == pl.num_programs(0) - 1)
        def _():
            for side in range(2):
                cross = sums[3 + side]
                whole = sums[side] + cross + cross.T
                packed[5 * side] = whole[:LANES, :LANES]
                packed[5 * side + 1] = whole[LANES:, :LANES]
                packed[5 * side + 2] = whole[LANES:, LANES:]
            packed[3] = sums[2, :LANES, :LANES]
            packed[4] = sums[2, LANES:, :LANES]
            packed[8] = sums[2, :LANES, LANES:]
            packed[9] = sums[2, LANES:, LANES:]


BLOCKS = ((0, 0), (1, 0), (1, 1), (2, 0), (3, 0), (2, 2), (3, 2), (3, 3), (2, 1), (3, 1))


def gram_chunk(chunk, place, blocks, pieces, mean, carried):
    rows = pieces[0].shape[0]
    steps = rows // TILE
    pixels, width = blocks.shape[1], 4 * LANES
    first, last = chunk == 0, chunk == CHUNKS - 1
    at = chunk * steps
    piece = pl.BlockSpec((TILE, LANES), lambda t, y: (t, 0))
    whole = pl.BlockSpec((5, 256, 256), lambda t, y: (0, 0, 0))
    half = pl.BlockSpec((TILE, width), lambda t, y: (t + at, 0))
    in_specs = [
        pl.BlockSpec((1, TILE, LANES), lambda t, y: (y[0], t + at, 0)),
        piece,
        piece,
        piece,
        pl.BlockSpec((1, width), lambda t, y: (0, 0)),
    ]
    args = [place, blocks, *pieces, mean]
    aliases = {}
    if not first:
        high, low, sums = carried
        in_specs += [whole, pl.BlockSpec(memory_space=pl.ANY), pl.BlockSpec(memory_space=pl.ANY)]
        args += [sums, high, low]
        aliases = {6: 2, 7: 0, 8: 1}
    out_specs = [half, half, whole]
    out_shape = [
        jax.ShapeDtypeStruct((pixels, width), jnp.bfloat16),
        jax.ShapeDtypeStruct((pixels, width), jnp.bfloat16),
        jax.ShapeDtypeStruct((5, 256, 256), jnp.float32),
    ]
    if last:
        out_specs.append(pl.BlockSpec((10, LANES, LANES), lambda t, y: (0, 0, 0)))
        out_shape.append(jax.ShapeDtypeStruct((10, LANES, LANES), jnp.float32))
    return pl.pallas_call(
        functools.partial(gram_kernel, last, first),
        grid_spec=pltpu.PrefetchScalarGridSpec(
            num_scalar_prefetch=1, grid=(steps,), in_specs=in_specs, out_specs=out_specs
        ),
        out_shape=out_shape,
        input_output_aliases=aliases,
        compiler_params=pltpu.CompilerParams(vmem_limit_bytes=VMEM_LIMIT),
        cost_estimate=pl.CostEstimate(
            flops=7 * 2 * rows * 256 * 256, bytes_accessed=rows * width * 8, transcendentals=0
        ),
        name="gram",
    )(*args)


def factor_block(rest, carried):
    outs = []
    row = lax.broadcasted_iota(jnp.int32, (8, LANES), 0)
    for at in range(0, LANES, 8):
        rows = LANES - at
        columns = [jnp.broadcast_to(rest[:, at + c : at + c + 1], (rows, LANES)) for c in range(8)]
        scale = jnp.zeros((8, LANES), jnp.float32)
        for j in range(8):
            pivot = columns[j][j : j + 1, :]
            scale = jnp.where(row == j, lax.rsqrt(jnp.broadcast_to(pivot, (8, LANES))), scale)
            weight = columns[j] * (1.0 / pivot)
            inside = jnp.where(row > j, weight[:8], 0.0)
            weight = jnp.concatenate([inside, weight[8:]], axis=0) if rows > 8 else inside
            for c in range(j + 1, 8):
                columns[c] = columns[c] - weight * columns[c][j : j + 1, :]
            rest = rest - weight * rest[j : j + 1, :]
            carried = carried - weight * carried[j : j + 1, :]
        outs.append(carried[:8] * scale)
        rest, carried = rest[8:], carried[8:]
    return jnp.concatenate(outs, axis=0)


def factor_kernel(pixels, packed, high, low, spread, gram, inverse):
    n = gram.shape[0]
    shape = (LANES, LANES)
    eye = lax.broadcasted_iota(jnp.int32, shape, 0) == lax.broadcasted_iota(jnp.int32, shape, 1)
    across, down = [], []
    for k in range(4):
        index = BLOCKS.index((k, k))
        diagonal = jnp.where(eye, packed[index], 0.0) * (1.0 / pixels)
        flat = jnp.sum(diagonal, axis=0, keepdims=True)
        spread[0:1, k * LANES : (k + 1) * LANES] = flat
        across.append(lax.rsqrt(flat + 1e-05))
        down.append(lax.rsqrt(jnp.sum(diagonal, axis=1, keepdims=True) + 1e-05))
    for index, (i, j) in enumerate(BLOCKS):
        block = packed[index] * (1.0 / pixels) * down[i] * across[j]
        gram[i * LANES : (i + 1) * LANES, j * LANES : (j + 1) * LANES] = block
        if i != j:
            gram[j * LANES : (j + 1) * LANES, i * LANES : (i + 1) * LANES] = block.T
    plain = ((1,), (0,))
    for at in range(0, n, LANES):
        end = at + LANES
        here = slice(at, end)
        own = factor_block(gram[here, here], jnp.where(eye, 1.0, 0.0))
        if at > 0:
            inverse[here, :at] = dot(own, inverse[here, :at], plain, EXACT)
        inverse[here, here] = own
        if end < n:
            inverse[here, end:] = jnp.zeros((LANES, n - end), jnp.float32)
            right = dot(own, gram[here, end:], plain, EXACT)
            down_side = right.T
            gram[end:, end:] -= dot(down_side, right, plain, EXACT)
            moved = dot(down_side, inverse[here, :end], plain, EXACT)
            if at > 0:
                inverse[end:, :at] -= moved[:, :at]
            inverse[end:, here] = -moved[:, at:]
    scaled = inverse[...] * jnp.concatenate(across, axis=1)
    top = scaled.astype(jnp.bfloat16)
    high[...] = top
    low[...] = (scaled - top.astype(jnp.float32)).astype(jnp.bfloat16)


def factor(packed, pixels):
    n = 4 * LANES
    vmem = pl.BlockSpec(memory_space=pltpu.VMEM)
    return pl.pallas_call(
        functools.partial(factor_kernel, pixels),
        in_specs=[vmem],
        out_specs=[vmem, vmem, vmem],
        out_shape=[
            jax.ShapeDtypeStruct((n, n), jnp.bfloat16),
            jax.ShapeDtypeStruct((n, n), jnp.bfloat16),
            jax.ShapeDtypeStruct((1, n), jnp.float32),
        ],
        scratch_shapes=[pltpu.VMEM((n, n), jnp.float32), pltpu.VMEM((n, n), jnp.float32)],
        compiler_params=pltpu.CompilerParams(vmem_limit_bytes=VMEM_LIMIT),
        name="factor",
    )(packed)


def scores_kernel(high, low, factor_high, factor_low, out):
    half = 2 * LANES
    lanes = ((1,), (1,))
    for part in range(2):
        depth, cols = (part + 1) * half, slice(part * half, (part + 1) * half)
        a, al = high[:, :depth], low[:, :depth]
        f, fl = factor_high[cols, :depth], factor_low[cols, :depth]
        out[:, cols] = dot(a, f, lanes) + dot(al, f, lanes) + dot(a, fl, lanes)


def scores_of(high, low, factor_high, factor_low):
    pixels, n = high.shape
    tile = pl.BlockSpec((TILE, n), lambda t: (t, 0))
    whole = pl.BlockSpec((n, n), lambda t: (0, 0))
    return pl.pallas_call(
        scores_kernel,
        grid=(pixels // TILE,),
        in_specs=[tile, tile, whole, whole],
        out_specs=tile,
        out_shape=jax.ShapeDtypeStruct((pixels, n), jnp.float32),
        compiler_params=pltpu.CompilerParams(vmem_limit_bytes=VMEM_LIMIT),
        name="scores",
    )(high, low, factor_high, factor_low)


def shifted(value, axis, away):
    size = lax.axis_size(axis)
    return lax.ppermute(value, axis, [(k, (k + away) % size) for k in range(size)])


def swapped(value, axis, mask):
    return lax.ppermute(value, axis, [(k, k ^ mask) for k in range(lax.axis_size(axis))])


def summed(packed):
    core = lax.axis_index("core")
    blocks = packed.shape[0]
    half = packed.reshape(2, blocks // 2, LANES, LANES)
    mine = lax.dynamic_index_in_dim(half, core, 0, False)
    other = lax.dynamic_index_in_dim(half, 1 - core, 0, False)
    mine = mine + swapped(other, "core", 1)
    share = mine.reshape(16, -1, LANES)
    part = jnp.sum(lax.all_to_all(share, ("x", "z"), 0, 0), axis=0)
    part = swapped(part, "y", 1) + part
    part = swapped(part, "y", 2) + part
    spread = jnp.broadcast_to(part, share.shape)
    mine = lax.all_to_all(spread, ("x", "z"), 0, 0).reshape(mine.shape)
    other = swapped(mine, "core", 1)
    pair = jnp.where(core == 0, jnp.stack([mine, other]), jnp.stack([other, mine]))
    return pair.reshape(packed.shape)


def body(pixel_stack):
    y = lax.axis_index("y")
    lay = lax.axis_size("y")
    pixels = pixel_stack.shape[0] * 32
    blocks = pixel_stack.reshape(lay, -1, LANES)
    rows = blocks.shape[1] // CHUNKS
    arrived = []
    for chunk in range(CHUNKS):
        pieces = []
        for away in range(1, lay):
            sent = lax.dynamic_slice(
                blocks, (lax.rem(y + away, lay), chunk * rows, 0), (1, rows, LANES)
            ).reshape(rows, LANES)
            pieces.append(shifted(sent, "y", away))
        arrived.append(pieces)

    total = jnp.sum(pixel_stack, axis=0, keepdims=True)
    for axis, mask in (("core", 1), ("x", 1), ("x", 2), ("z", 1), ("z", 2)):
        total = total + swapped(total, axis, mask)
    mean = total / pixels
    means = jnp.zeros((1, lay * LANES), jnp.float32)
    for away in range(lay):
        value = mean if away == 0 else shifted(mean, "y", away)
        means = lax.dynamic_update_slice(means, value, (0, lax.rem(y - away + lay, lay) * LANES))

    place = y.astype(jnp.int32).reshape(1)
    carried = None
    for chunk in range(CHUNKS):
        *carried, packed = [
            *gram_chunk(chunk, place, blocks, arrived[chunk], means, carried),
            *([] if chunk == CHUNKS - 1 else [None]),
        ]
    high, low, _ = carried
    factor_high, factor_low, spread = factor(summed(packed), pixels)
    scores = scores_of(high, low, factor_high, factor_low)
    own = lax.dynamic_slice(spread, (0, y * LANES), (1, LANES)).reshape(LANES)
    return scores, 0.5 * jnp.log(own + 1e-05)


def solution(mesh):
    devices = mesh.devices.reshape(4, 4, 2, 4)
    fine = Mesh(devices, ("x", "z", "core", "y"))
    return jax.shard_map(
        body,
        mesh=fine,
        in_specs=(P(("x", "z", "core"), "y"),),
        out_specs=(P(("x", "z", "core", "y"), None), P("y")),
        check_vma=False,
    )
```

```python
import functools

import jax
import jax.numpy as jnp
from jax import lax
from jax.experimental import pallas as pl
from jax.experimental.pallas import tpu as pltpu
from jax.sharding import Mesh
from jax.sharding import PartitionSpec as P

EXACT = lax.Precision.HIGHEST
LANES = 128
CHUNKS = (512, 512, 2560, 512)
TILE = 512
VMEM_LIMIT = 56 * 2**20


def dot(a, b, contract, precision=None):
    return lax.dot_general(
        a, b, (contract, ((), ())), precision=precision, preferred_element_type=jnp.float32
    )


def gram_kernel(last, first, place, own, near, far, back, mean, *rest):
    rest = list(rest)
    held = None if first else rest.pop(0)
    if not first:
        rest.pop(0), rest.pop(0)
    high, low, sums = rest[:3]
    packed = rest[3] if last else None
    step = pl.program_id(0)

    @pl.when(step == 0)
    def _():
        sums[...] = jnp.zeros_like(sums) if first else held[...]

    for away, ref in enumerate((own, near, far, back)):
        layer = lax.rem(place[0] - away + 4, 4)
        lanes = pl.ds(pl.multiple_of(layer * LANES, LANES), LANES)
        value = ref[...].reshape(-1, LANES) - mean[0:1, lanes]
        top = value.astype(jnp.bfloat16)
        high[:, lanes] = top
        low[:, lanes] = (value - top.astype(jnp.float32)).astype(jnp.bfloat16)

    rows = ((0,), (0,))
    half = 2 * LANES
    a, b = high[:, :half], high[:, half:]
    al, bl = low[:, :half], low[:, half:]
    sums[0] += dot(a, a, rows)
    sums[1] += dot(b, b, rows)
    sums[2] += dot(b, a, rows) + dot(b, al, rows) + dot(bl, a, rows)
    sums[3] += dot(a, al, rows)
    sums[4] += dot(b, bl, rows)

    if last:

        @pl.when(step == pl.num_programs(0) - 1)
        def _():
            for side in range(2):
                cross = sums[3 + side]
                whole = sums[side] + cross + cross.T
                packed[5 * side] = whole[:LANES, :LANES]
                packed[5 * side + 1] = whole[LANES:, :LANES]
                packed[5 * side + 2] = whole[LANES:, LANES:]
            packed[3] = sums[2, :LANES, :LANES]
            packed[4] = sums[2, LANES:, :LANES]
            packed[8] = sums[2, :LANES, LANES:]
            packed[9] = sums[2, LANES:, LANES:]


BLOCKS = ((0, 0), (1, 0), (1, 1), (2, 0), (3, 0), (2, 2), (3, 2), (3, 3), (2, 1), (3, 1))


def gram_chunk(chunk, place, blocks, pieces, mean, carried):
    rows = CHUNKS[chunk]
    steps = rows // TILE
    pixels, width = blocks.shape[1], 4 * LANES
    first, last = chunk == 0, chunk == len(CHUNKS) - 1
    at = sum(CHUNKS[:chunk]) // TILE
    piece = pl.BlockSpec((TILE, LANES), lambda t, y: (t, 0))
    whole = pl.BlockSpec((5, 256, 256), lambda t, y: (0, 0, 0))
    half = pl.BlockSpec((TILE, width), lambda t, y: (t + at, 0))
    in_specs = [
        pl.BlockSpec((1, TILE, LANES), lambda t, y: (y[0], t + at, 0)),
        piece,
        piece,
        piece,
        pl.BlockSpec((1, width), lambda t, y: (0, 0)),
    ]
    args = [place, blocks, *pieces, mean]
    aliases = {}
    if not first:
        high, low, sums = carried
        in_specs += [whole, pl.BlockSpec(memory_space=pl.ANY), pl.BlockSpec(memory_space=pl.ANY)]
        args += [sums, high, low]
        aliases = {6: 2, 7: 0, 8: 1}
    out_specs = [half, half, whole]
    out_shape = [
        jax.ShapeDtypeStruct((pixels, width), jnp.bfloat16),
        jax.ShapeDtypeStruct((pixels, width), jnp.bfloat16),
        jax.ShapeDtypeStruct((5, 256, 256), jnp.float32),
    ]
    if last:
        out_specs.append(pl.BlockSpec((10, LANES, LANES), lambda t, y: (0, 0, 0)))
        out_shape.append(jax.ShapeDtypeStruct((10, LANES, LANES), jnp.float32))
    return pl.pallas_call(
        functools.partial(gram_kernel, last, first),
        grid_spec=pltpu.PrefetchScalarGridSpec(
            num_scalar_prefetch=1, grid=(steps,), in_specs=in_specs, out_specs=out_specs
        ),
        out_shape=out_shape,
        input_output_aliases=aliases,
        compiler_params=pltpu.CompilerParams(vmem_limit_bytes=VMEM_LIMIT),
        cost_estimate=pl.CostEstimate(
            flops=7 * 2 * rows * 256 * 256, bytes_accessed=rows * width * 8, transcendentals=0
        ),
        name="gram",
    )(*args)


def factor_block(rest, carried, beside):
    outs = []
    row = lax.broadcasted_iota(jnp.int32, (8, LANES), 0)
    for at in range(0, LANES, 8):
        rows = LANES - at
        columns = [jnp.broadcast_to(rest[:, at + c : at + c + 1], (rows, LANES)) for c in range(8)]
        scale = jnp.zeros((8, LANES), jnp.float32)
        for j in range(8):
            pivot = columns[j][j : j + 1, :]
            scale = jnp.where(row == j, lax.rsqrt(jnp.broadcast_to(pivot, (8, LANES))), scale)
            weight = columns[j] * (1.0 / pivot)
            inside = jnp.where(row > j, weight[:8], 0.0)
            weight = jnp.concatenate([inside, weight[8:]], axis=0) if rows > 8 else inside
            for c in range(j + 1, 8):
                columns[c] = columns[c] - weight * columns[c][j : j + 1, :]
            rest = rest - weight * rest[j : j + 1, :]
            carried = carried - weight * carried[j : j + 1, :]
        outs.append(carried[:8] * scale)
        rest, carried = rest[8:], carried[8:]
        beside(at // 8)
    return jnp.concatenate(outs, axis=0)


def whiten_kernel(pixels, packed, high_hbm, low_hbm, scores_hbm, spread, *scratch):
    high, low, out, gram, inverse, both, in_sems, out_sems = scratch
    n = gram.shape[0]
    fetches = [
        pltpu.make_async_copy(high_hbm, high, in_sems.at[0]),
        pltpu.make_async_copy(low_hbm, low, in_sems.at[1]),
    ]
    for fetch in fetches:
        fetch.start()

    shape = (LANES, LANES)
    eye = lax.broadcasted_iota(jnp.int32, shape, 0) == lax.broadcasted_iota(jnp.int32, shape, 1)
    across, down = [], []
    for k in range(4):
        index = BLOCKS.index((k, k))
        diagonal = jnp.where(eye, packed[index], 0.0) * (1.0 / pixels)
        flat = jnp.sum(diagonal, axis=0, keepdims=True)
        spread[0:1, k * LANES : (k + 1) * LANES] = flat
        across.append(lax.rsqrt(flat + 1e-05))
        down.append(lax.rsqrt(jnp.sum(diagonal, axis=1, keepdims=True) + 1e-05))
    for index, (i, j) in enumerate(BLOCKS):
        block = packed[index] * (1.0 / pixels) * down[i] * across[j]
        gram[i * LANES : (i + 1) * LANES, j * LANES : (j + 1) * LANES] = block
        if i != j:
            gram[j * LANES : (j + 1) * LANES, i * LANES : (i + 1) * LANES] = block.T

    plain, lanes = ((1,), (0,)), ((1,), (1,))
    pieces = 16
    rows = high.shape[0] // pieces
    sends = []

    def score(column, piece):
        depth = (column + 1) * LANES
        here = slice(piece * rows, (piece + 1) * rows)
        cols = slice(column * LANES, (column + 1) * LANES)
        wide = dot(high[here, :depth], both[:, :depth], lanes)
        narrow = dot(low[here, :depth], both[:LANES, :depth], lanes)
        out[here, cols] = wide[:, :LANES] + wide[:, LANES:] + narrow
        if piece % 4 == 3:
            done = slice((piece - 3) * rows, (piece + 1) * rows)
            send = pltpu.make_async_copy(
                out.at[done, cols], scores_hbm.at[done, cols], out_sems.at[len(sends)]
            )
            send.start()
            sends.append(send)

    for column in range(4):
        at = column * LANES
        end = at + LANES
        here = slice(at, end)
        if column == 1:
            for fetch in fetches:
                fetch.wait()
        beside = (lambda piece: score(column - 1, piece)) if column else (lambda piece: None)
        own = factor_block(gram[here, here], jnp.where(eye, 1.0, 0.0), beside)
        if at > 0:
            inverse[here, :at] = dot(own, inverse[here, :at], plain, EXACT)
        inverse[here, here] = own
        if end < n:
            right = dot(own, gram[here, end:], plain, EXACT)
            down_side = right.T
            gram[end:, end:] -= dot(down_side, right, plain, EXACT)
            moved = dot(down_side, inverse[here, :end], plain, EXACT)
            if at > 0:
                inverse[end:, :at] -= moved[:, :at]
            inverse[end:, here] = -moved[:, at:]
        scaled = inverse[here, :end] * jnp.concatenate(across[: column + 1], axis=1)
        top = scaled.astype(jnp.bfloat16)
        both[:LANES, :end] = top
        both[LANES:, :end] = (scaled - top.astype(jnp.float32)).astype(jnp.bfloat16)
    for piece in range(pieces):
        score(3, piece)
    for send in sends:
        send.wait()


def whiten(packed, high, low, pixels):
    rows, n = high.shape
    vmem, hbm = pl.BlockSpec(memory_space=pltpu.VMEM), pl.BlockSpec(memory_space=pl.ANY)
    return pl.pallas_call(
        functools.partial(whiten_kernel, pixels),
        in_specs=[vmem, hbm, hbm],
        out_specs=[hbm, vmem],
        out_shape=[
            jax.ShapeDtypeStruct((rows, n), jnp.float32),
            jax.ShapeDtypeStruct((1, n), jnp.float32),
        ],
        scratch_shapes=[
            pltpu.VMEM((rows, n), jnp.bfloat16),
            pltpu.VMEM((rows, n), jnp.bfloat16),
            pltpu.VMEM((rows, n), jnp.float32),
            pltpu.VMEM((n, n), jnp.float32),
            pltpu.VMEM((n, n), jnp.float32),
            pltpu.VMEM((2 * LANES, n), jnp.bfloat16),
            pltpu.SemaphoreType.DMA((2,)),
            pltpu.SemaphoreType.DMA((16,)),
        ],
        compiler_params=pltpu.CompilerParams(vmem_limit_bytes=VMEM_LIMIT),
        name="whiten",
    )(packed, high, low)


def shifted(value, axis, away):
    size = lax.axis_size(axis)
    return lax.ppermute(value, axis, [(k, (k + away) % size) for k in range(size)])


def swapped(value, axis, mask):
    return lax.ppermute(value, axis, [(k, k ^ mask) for k in range(lax.axis_size(axis))])


def summed(packed):
    core = lax.axis_index("core")
    blocks = packed.shape[0]
    half = packed.reshape(2, blocks // 2, LANES, LANES)
    mine = lax.dynamic_index_in_dim(half, core, 0, False)
    other = lax.dynamic_index_in_dim(half, 1 - core, 0, False)
    mine = mine + swapped(other, "core", 1)
    share = mine.reshape(16, -1, LANES)
    part = jnp.sum(lax.all_to_all(share, ("x", "z"), 0, 0), axis=0)
    part = swapped(part, "y", 1) + part
    part = swapped(part, "y", 2) + part
    spread = jnp.broadcast_to(part, share.shape)
    mine = lax.all_to_all(spread, ("x", "z"), 0, 0).reshape(mine.shape)
    other = swapped(mine, "core", 1)
    pair = jnp.where(core == 0, jnp.stack([mine, other]), jnp.stack([other, mine]))
    return pair.reshape(packed.shape)


def body(pixel_stack):
    y = lax.axis_index("y")
    lay = lax.axis_size("y")
    pixels = pixel_stack.shape[0] * 32
    blocks = pixel_stack.reshape(lay, -1, LANES)

    def picked(source, chunk, away):
        rows = CHUNKS[chunk]
        start = (lax.rem(y + away, lay), sum(CHUNKS[:chunk]), 0)
        return lax.dynamic_slice(source, start, (1, rows, LANES)).reshape(rows, LANES)

    first = [picked(blocks, 0, away) for away in range(1, lay)]
    stack, _ = lax.optimization_barrier((pixel_stack, first))
    arrived = [[shifted(piece, "y", away) for away, piece in enumerate(first, 1)]]
    total = jnp.sum(stack, axis=0, keepdims=True)
    tail = jnp.broadcast_to(total, (8, LANES))
    pieces = [jnp.concatenate([picked(blocks, 1, away), tail], axis=0) for away in range(1, lay)]
    arrived.append([shifted(piece, "y", away) for away, piece in enumerate(pieces, 1)])
    for chunk in range(2, len(CHUNKS)):
        later, arrived[chunk - 2] = lax.optimization_barrier((blocks, arrived[chunk - 2]))
        arrived.append(
            [shifted(picked(later, chunk, away), "y", away) for away in range(1, lay)]
        )

    sums = jnp.zeros((1, lay * LANES), jnp.float32)
    for away in range(lay):
        value = total if away == 0 else arrived[1][away - 1][-8:-7]
        sums = lax.dynamic_update_slice(sums, value, (0, lax.rem(y - away + lay, lay) * LANES))
    sums = lax.all_to_all(jnp.broadcast_to(sums, (32, 1, lay * LANES)), ("x", "z", "core"), 0, 0)
    means = jnp.sum(sums, axis=0) / pixels

    place = y.astype(jnp.int32).reshape(1)
    carried = None
    for chunk, pieces in enumerate(arrived):
        carried = gram_chunk(chunk, place, blocks, pieces, means, carried)
    high, low, _, packed = carried
    scores, spread = whiten(summed(packed), high, low, pixels)
    own = lax.dynamic_slice(spread, (0, y * LANES), (1, LANES)).reshape(LANES)
    return scores, 0.5 * jnp.log(own + 1e-05)


def solution(mesh):
    devices = mesh.devices.reshape(4, 4, 2, 4)
    fine = Mesh(devices, ("x", "z", "core", "y"))
    return jax.shard_map(
        body,
        mesh=fine,
        in_specs=(P(("x", "z", "core"), "y"),),
        out_specs=(P(("x", "z", "core", "y"), None), P("y")),
        check_vma=False,
    )
```

```python
import functools

import jax
import jax.numpy as jnp
from jax import lax
from jax.experimental import pallas as pl
from jax.experimental.pallas import tpu as pltpu
from jax.sharding import Mesh
from jax.sharding import PartitionSpec as P

EXACT = lax.Precision.HIGHEST
LANES = 128
CHUNKS = (512, 512, 2560, 512)
TILE = 512
PANEL = 64
VMEM_LIMIT = 56 * 2**20


def dot(a, b, contract, precision=None):
    return lax.dot_general(
        a, b, (contract, ((), ())), precision=precision, preferred_element_type=jnp.float32
    )


def gram_kernel(last, first, place, own, near, far, back, mean, *rest):
    rest = list(rest)
    held = None if first else rest.pop(0)
    if not first:
        rest.pop(0), rest.pop(0)
    high, low, sums = rest[:3]
    mine, other = rest[3:] if last else (None, None)
    step = pl.program_id(0)

    @pl.when(step == 0)
    def _():
        sums[...] = jnp.zeros_like(sums) if first else held[...]

    for away, ref in enumerate((own, near, far, back)):
        layer = lax.rem(place[0] - away + 4, 4)
        lanes = pl.ds(pl.multiple_of(layer * LANES, LANES), LANES)
        value = ref[...].reshape(-1, LANES) - mean[0:1, lanes]
        top = value.astype(jnp.bfloat16)
        high[:, lanes] = top
        low[:, lanes] = (value - top.astype(jnp.float32)).astype(jnp.bfloat16)

    rows = ((0,), (0,))
    half = 2 * LANES
    a, b = high[:, :half], high[:, half:]
    al, bl = low[:, :half], low[:, half:]
    sums[0] += dot(a, a, rows)
    sums[1] += dot(b, b, rows)
    sums[2] += dot(b, a, rows) + dot(b, al, rows) + dot(bl, a, rows)
    sums[3] += dot(a, al, rows)
    sums[4] += dot(b, bl, rows)

    if last:

        @pl.when(step == pl.num_programs(0) - 1)
        def _():
            packed = {}
            for side in range(2):
                cross = sums[3 + side]
                whole = sums[side] + cross + cross.T
                packed[5 * side] = whole[:LANES, :LANES]
                packed[5 * side + 1] = whole[LANES:, :LANES]
                packed[5 * side + 2] = whole[LANES:, LANES:]
            packed[3] = sums[2, :LANES, :LANES]
            packed[4] = sums[2, LANES:, :LANES]
            packed[8] = sums[2, :LANES, LANES:]
            packed[9] = sums[2, LANES:, LANES:]
            for block in range(5):
                low_half = place[1] == 0
                mine[block] = jnp.where(low_half, packed[block], packed[5 + block])
                other[block] = jnp.where(low_half, packed[5 + block], packed[block])


BLOCKS = ((0, 0), (1, 0), (1, 1), (2, 0), (3, 0), (2, 2), (3, 2), (3, 3), (2, 1), (3, 1))


def gram_chunk(chunk, place, blocks, pieces, mean, carried):
    rows = CHUNKS[chunk]
    steps = rows // TILE
    pixels, width = blocks.shape[1], 4 * LANES
    first, last = chunk == 0, chunk == len(CHUNKS) - 1
    at = sum(CHUNKS[:chunk]) // TILE
    piece = pl.BlockSpec((TILE, LANES), lambda t, y: (t, 0))
    whole = pl.BlockSpec((5, 256, 256), lambda t, y: (0, 0, 0))
    half = pl.BlockSpec((TILE, width), lambda t, y: (t + at, 0))
    in_specs = [
        pl.BlockSpec((1, TILE, LANES), lambda t, y: (y[0], t + at, 0)),
        piece,
        piece,
        piece,
        pl.BlockSpec((1, width), lambda t, y: (0, 0)),
    ]
    args = [place, blocks, *pieces, mean]
    aliases = {}
    if not first:
        high, low, sums = carried
        in_specs += [whole, pl.BlockSpec(memory_space=pl.ANY), pl.BlockSpec(memory_space=pl.ANY)]
        args += [sums, high, low]
        aliases = {6: 2, 7: 0, 8: 1}
    out_specs = [half, half, whole]
    out_shape = [
        jax.ShapeDtypeStruct((pixels, width), jnp.bfloat16),
        jax.ShapeDtypeStruct((pixels, width), jnp.bfloat16),
        jax.ShapeDtypeStruct((5, 256, 256), jnp.float32),
    ]
    if last:
        out_specs += [pl.BlockSpec((5, LANES, LANES), lambda t, y: (0, 0, 0))] * 2
        out_shape += [jax.ShapeDtypeStruct((5, LANES, LANES), jnp.float32)] * 2
    return pl.pallas_call(
        functools.partial(gram_kernel, last, first),
        grid_spec=pltpu.PrefetchScalarGridSpec(
            num_scalar_prefetch=1, grid=(steps,), in_specs=in_specs, out_specs=out_specs
        ),
        out_shape=out_shape,
        input_output_aliases=aliases,
        compiler_params=pltpu.CompilerParams(vmem_limit_bytes=VMEM_LIMIT),
        cost_estimate=pl.CostEstimate(
            flops=7 * 2 * rows * 256 * 256, bytes_accessed=rows * width * 8, transcendentals=0
        ),
        name="gram",
    )(*args)


def eliminate(rest, carried, first, beside):
    kept, factor = [], []
    row = lax.broadcasted_iota(jnp.int32, (8, LANES), 0)
    for at in range(first, first + PANEL, 8):
        rows = rest.shape[0]
        columns = [jnp.broadcast_to(rest[:, at + c : at + c + 1], (rows, LANES)) for c in range(8)]
        scale = jnp.zeros((8, LANES), jnp.float32)
        for j in range(8):
            root = lax.rsqrt(columns[j][j : j + 1, :])
            scale = jnp.where(row == j, jnp.broadcast_to(root, (8, LANES)), scale)
            weight = columns[j] * (root * root)
            inside = jnp.where(row > j, weight[:8], 0.0)
            weight = jnp.concatenate([inside, weight[8:]], axis=0) if rows > 8 else inside
            for c in range(j + 1, 8):
                columns[c] = columns[c] - weight * columns[c][j : j + 1, :]
            rest = rest - weight * rest[j : j + 1, :]
            carried = carried - weight * carried[j : j + 1, :]
        kept.append(rest[:8] * scale)
        factor.append(carried[:8] * scale)
        rest, carried = rest[8:], carried[8:]
        beside(at // 8)
    return jnp.concatenate(kept, axis=0), jnp.concatenate(factor, axis=0)


def factor_block(rest, carried, beside):
    outs = []
    for first in range(0, LANES, PANEL):
        kept, factor = eliminate(rest[:PANEL], carried[:PANEL], first, beside)
        outs.append(factor)
        if first + PANEL < LANES:
            below = kept.T[first + PANEL :]
            both = jnp.concatenate([kept, factor], axis=1)
            moved = dot(below, both, ((1,), (0,)), EXACT)
            rest, carried = rest[PANEL:] - moved[:, :LANES], carried[PANEL:] - moved[:, LANES:]
    return jnp.concatenate(outs, axis=0)


def whiten_kernel(pixels, place, mine, other, high_hbm, low_hbm, scores_hbm, log_scale, *scratch):
    high, low, out, gram, inverse, both, in_sems, out_sems = scratch
    n = gram.shape[0]
    fetches = [
        pltpu.make_async_copy(high_hbm, high, in_sems.at[0]),
        pltpu.make_async_copy(low_hbm, low, in_sems.at[1]),
    ]
    for fetch in fetches:
        fetch.start()

    def packed(index):
        side, block = divmod(index, 5)
        return jnp.where(place[1] == side, mine[block], other[block])

    shape = (LANES, LANES)
    eye = lax.broadcasted_iota(jnp.int32, shape, 0) == lax.broadcasted_iota(jnp.int32, shape, 1)
    across, down = [], []
    spread = jnp.zeros((1, LANES), jnp.float32)
    for k in range(4):
        index = BLOCKS.index((k, k))
        diagonal = jnp.where(eye, packed(index), 0.0) * (1.0 / pixels)
        flat = jnp.sum(diagonal, axis=0, keepdims=True)
        spread = spread + jnp.where(place[0] == k, flat, 0.0)
        across.append(lax.rsqrt(flat + 1e-05))
        down.append(lax.rsqrt(jnp.sum(diagonal, axis=1, keepdims=True) + 1e-05))
    for index, (i, j) in enumerate(BLOCKS):
        block = packed(index) * (1.0 / pixels) * down[i] * across[j]
        gram[i * LANES : (i + 1) * LANES, j * LANES : (j + 1) * LANES] = block
        if i != j:
            gram[j * LANES : (j + 1) * LANES, i * LANES : (i + 1) * LANES] = block.T

    log_scale[...] = 0.5 * jnp.log(spread + 1e-05)
    plain, lanes = ((1,), (0,)), ((1,), (1,))
    pieces = 16
    rows = high.shape[0] // pieces
    sends = []

    def score(column, piece):
        depth = (column + 1) * LANES
        here = slice(piece * rows, (piece + 1) * rows)
        cols = slice(column * LANES, (column + 1) * LANES)
        wide = dot(high[here, :depth], both[:, :depth], lanes)
        narrow = dot(low[here, :depth], both[:LANES, :depth], lanes)
        out[here, cols] = wide[:, :LANES] + wide[:, LANES:] + narrow
        if piece % 4 == 3:
            done = slice((piece - 3) * rows, (piece + 1) * rows)
            send = pltpu.make_async_copy(
                out.at[done, cols], scores_hbm.at[done, cols], out_sems.at[len(sends)]
            )
            send.start()
            sends.append(send)

    for column in range(4):
        at = column * LANES
        end = at + LANES
        here = slice(at, end)
        if column == 1:
            for fetch in fetches:
                fetch.wait()
        beside = (lambda piece: score(column - 1, piece)) if column else (lambda piece: None)
        own = factor_block(gram[here, here], jnp.where(eye, 1.0, 0.0), beside)
        if at > 0:
            inverse[here, :at] = dot(own, inverse[here, :at], plain, EXACT)
        inverse[here, here] = own
        if end < n:
            right = dot(own, gram[here, end:], plain, EXACT)
            down_side = right.T
            gram[end:, end:] -= dot(down_side, right, plain, EXACT)
            moved = dot(down_side, inverse[here, :end], plain, EXACT)
            if at > 0:
                inverse[end:, :at] -= moved[:, :at]
            inverse[end:, here] = -moved[:, at:]
        scaled = inverse[here, :end] * jnp.concatenate(across[: column + 1], axis=1)
        top = scaled.astype(jnp.bfloat16)
        both[:LANES, :end] = top
        both[LANES:, :end] = (scaled - top.astype(jnp.float32)).astype(jnp.bfloat16)
    for piece in range(pieces):
        score(3, piece)
    for send in sends:
        send.wait()


def whiten(place, mine, other, high, low, pixels):
    rows, n = high.shape
    vmem, hbm = pl.BlockSpec(memory_space=pltpu.VMEM), pl.BlockSpec(memory_space=pl.ANY)
    return pl.pallas_call(
        functools.partial(whiten_kernel, pixels),
        in_specs=[pl.BlockSpec(memory_space=pltpu.SMEM), vmem, vmem, hbm, hbm],
        out_specs=[hbm, vmem],
        out_shape=[
            jax.ShapeDtypeStruct((rows, n), jnp.float32),
            jax.ShapeDtypeStruct((1, LANES), jnp.float32),
        ],
        scratch_shapes=[
            pltpu.VMEM((rows, n), jnp.bfloat16),
            pltpu.VMEM((rows, n), jnp.bfloat16),
            pltpu.VMEM((rows, n), jnp.float32),
            pltpu.VMEM((n, n), jnp.float32),
            pltpu.VMEM((n, n), jnp.float32),
            pltpu.VMEM((2 * LANES, n), jnp.bfloat16),
            pltpu.SemaphoreType.DMA((2,)),
            pltpu.SemaphoreType.DMA((16,)),
        ],
        compiler_params=pltpu.CompilerParams(vmem_limit_bytes=VMEM_LIMIT),
        name="whiten",
    )(place, mine, other, high, low)


def shifted(value, axis, away):
    size = lax.axis_size(axis)
    return lax.ppermute(value, axis, [(k, (k + away) % size) for k in range(size)])


def swapped(value, axis, mask):
    return lax.ppermute(value, axis, [(k, k ^ mask) for k in range(lax.axis_size(axis))])


def summed(mine, other):
    mine = mine + swapped(other, "core", 1)
    share = mine.reshape(16, -1, LANES)
    part = jnp.sum(lax.all_to_all(share, ("x", "z"), 0, 0), axis=0)
    part = swapped(part, "y", 1) + part
    part = swapped(part, "y", 2) + part
    spread = jnp.broadcast_to(part, share.shape)
    mine = lax.all_to_all(spread, ("x", "z"), 0, 0).reshape(mine.shape)
    return mine, swapped(mine, "core", 1)


def body(pixel_stack):
    y = lax.axis_index("y")
    lay = lax.axis_size("y")
    pixels = pixel_stack.shape[0] * 32
    blocks = pixel_stack.reshape(lay, -1, LANES)

    def picked(source, chunk, away):
        rows = CHUNKS[chunk]
        start = (lax.rem(y + away, lay), sum(CHUNKS[:chunk]), 0)
        return lax.dynamic_slice(source, start, (1, rows, LANES)).reshape(rows, LANES)

    first = [picked(blocks, 0, away) for away in range(1, lay)]
    stack, _ = lax.optimization_barrier((pixel_stack, first))
    arrived = [[shifted(piece, "y", away) for away, piece in enumerate(first, 1)]]
    total = jnp.sum(stack, axis=0, keepdims=True)
    tail = jnp.broadcast_to(total, (8, LANES))
    pieces = [jnp.concatenate([picked(blocks, 1, away), tail], axis=0) for away in range(1, lay)]
    arrived.append([shifted(piece, "y", away) for away, piece in enumerate(pieces, 1)])
    for chunk in range(2, len(CHUNKS)):
        later, arrived[chunk - 2] = lax.optimization_barrier((blocks, arrived[chunk - 2]))
        arrived.append(
            [shifted(picked(later, chunk, away), "y", away) for away in range(1, lay)]
        )

    sums = jnp.zeros((1, lay * LANES), jnp.float32)
    for away in range(lay):
        value = total if away == 0 else arrived[1][away - 1][-8:-7]
        sums = lax.dynamic_update_slice(sums, value, (0, lax.rem(y - away + lay, lay) * LANES))
    sums = lax.all_to_all(jnp.broadcast_to(sums, (32, 1, lay * LANES)), ("x", "z", "core"), 0, 0)
    means = jnp.sum(sums, axis=0) / pixels

    place = jnp.stack([y, lax.axis_index("core")]).astype(jnp.int32)
    carried = None
    for chunk, pieces in enumerate(arrived):
        carried = gram_chunk(chunk, place, blocks, pieces, means, carried)
    high, low, _, mine, other = carried
    mine, other = summed(mine, other)
    scores, log_scale = whiten(place, mine, other, high, low, pixels)
    return scores, log_scale.reshape(LANES)


def solution(mesh):
    devices = mesh.devices.reshape(4, 4, 2, 4)
    fine = Mesh(devices, ("x", "z", "core", "y"))
    return jax.shard_map(
        body,
        mesh=fine,
        in_specs=(P(("x", "z", "core"), "y"),),
        out_specs=(P(("x", "z", "core", "y"), None), P("y")),
        check_vma=False,
    )
```

```python
import functools

import jax
import jax.numpy as jnp
from jax import lax
from jax.experimental import pallas as pl
from jax.experimental.pallas import tpu as pltpu
from jax.sharding import Mesh
from jax.sharding import PartitionSpec as P

EXACT = lax.Precision.HIGHEST
LANES = 128
CHUNKS = (512, 512, 2560, 512)
TILE = 512
PANEL = 64
VMEM_LIMIT = 56 * 2**20


def dot(a, b, contract, precision=None):
    return lax.dot_general(
        a, b, (contract, ((), ())), precision=precision, preferred_element_type=jnp.float32
    )


def gram_kernel(last, first, place, own, near, far, back, mean, *rest):
    rest = list(rest)
    held = None if first else rest.pop(0)
    if not first:
        rest.pop(0), rest.pop(0)
    high, low, sums = rest[:3]
    mine, other = rest[3:] if last else (None, None)
    step = pl.program_id(0)

    @pl.when(step == 0)
    def _():
        sums[...] = jnp.zeros_like(sums) if first else held[...]

    for away, ref in enumerate((own, near, far, back)):
        layer = lax.rem(place[0] - away + 4, 4)
        lanes = pl.ds(pl.multiple_of(layer * LANES, LANES), LANES)
        value = ref[...].reshape(-1, LANES) - mean[0:1, lanes]
        top = value.astype(jnp.bfloat16)
        high[:, lanes] = top
        low[:, lanes] = (value - top.astype(jnp.float32)).astype(jnp.bfloat16)

    rows = ((0,), (0,))
    half = 2 * LANES
    a, b = high[:, :half], high[:, half:]
    al, bl = low[:, :half], low[:, half:]
    sums[0] += dot(a, a, rows)
    sums[1] += dot(b, b, rows)
    sums[2] += dot(b, a, rows) + dot(b, al, rows) + dot(bl, a, rows)
    sums[3] += dot(a, al, rows)
    sums[4] += dot(b, bl, rows)

    if last:

        @pl.when(step == pl.num_programs(0) - 1)
        def _():
            packed = {}
            for side in range(2):
                cross = sums[3 + side]
                whole = sums[side] + cross + cross.T
                packed[5 * side] = whole[:LANES, :LANES]
                packed[5 * side + 1] = whole[LANES:, :LANES]
                packed[5 * side + 2] = whole[LANES:, LANES:]
            packed[3] = sums[2, :LANES, :LANES]
            packed[4] = sums[2, LANES:, :LANES]
            packed[8] = sums[2, :LANES, LANES:]
            packed[9] = sums[2, LANES:, LANES:]
            for block in range(5):
                low_half = place[1] == 0
                mine[block] = jnp.where(low_half, packed[block], packed[5 + block])
                other[block] = jnp.where(low_half, packed[5 + block], packed[block])


BLOCKS = ((0, 0), (1, 0), (1, 1), (2, 0), (3, 0), (2, 2), (3, 2), (3, 3), (2, 1), (3, 1))


def gram_chunk(chunk, place, blocks, pieces, mean, carried):
    rows = CHUNKS[chunk]
    steps = rows // TILE
    pixels, width = blocks.shape[1], 4 * LANES
    first, last = chunk == 0, chunk == len(CHUNKS) - 1
    at = sum(CHUNKS[:chunk]) // TILE
    piece = pl.BlockSpec((TILE, LANES), lambda t, y: (t, 0))
    whole = pl.BlockSpec((5, 256, 256), lambda t, y: (0, 0, 0))
    half = pl.BlockSpec((TILE, width), lambda t, y: (t + at, 0))
    in_specs = [
        pl.BlockSpec((1, TILE, LANES), lambda t, y: (y[0], t + at, 0)),
        piece,
        piece,
        piece,
        pl.BlockSpec((1, width), lambda t, y: (0, 0)),
    ]
    args = [place, blocks, *pieces, mean]
    aliases = {}
    if not first:
        high, low, sums = carried
        in_specs += [whole, pl.BlockSpec(memory_space=pl.ANY), pl.BlockSpec(memory_space=pl.ANY)]
        args += [sums, high, low]
        aliases = {6: 2, 7: 0, 8: 1}
    out_specs = [half, half, whole]
    out_shape = [
        jax.ShapeDtypeStruct((pixels, width), jnp.bfloat16),
        jax.ShapeDtypeStruct((pixels, width), jnp.bfloat16),
        jax.ShapeDtypeStruct((5, 256, 256), jnp.float32),
    ]
    if last:
        out_specs += [pl.BlockSpec((5, LANES, LANES), lambda t, y: (0, 0, 0))] * 2
        out_shape += [jax.ShapeDtypeStruct((5, LANES, LANES), jnp.float32)] * 2
    return pl.pallas_call(
        functools.partial(gram_kernel, last, first),
        grid_spec=pltpu.PrefetchScalarGridSpec(
            num_scalar_prefetch=1, grid=(steps,), in_specs=in_specs, out_specs=out_specs
        ),
        out_shape=out_shape,
        input_output_aliases=aliases,
        compiler_params=pltpu.CompilerParams(vmem_limit_bytes=VMEM_LIMIT),
        cost_estimate=pl.CostEstimate(
            flops=7 * 2 * rows * 256 * 256, bytes_accessed=rows * width * 8, transcendentals=0
        ),
        name="gram",
    )(*args)


def eliminate(rest, carried, first, beside):
    kept, factor = [], []
    row = lax.broadcasted_iota(jnp.int32, (8, LANES), 0)
    for at in range(first, first + PANEL, 8):
        rows = rest.shape[0]
        columns = [jnp.broadcast_to(rest[:, at + c : at + c + 1], (rows, LANES)) for c in range(8)]
        scale = jnp.zeros((8, LANES), jnp.float32)
        for j in range(8):
            root = lax.rsqrt(columns[j][j : j + 1, :])
            scale = jnp.where(row == j, jnp.broadcast_to(root, (8, LANES)), scale)
            weight = columns[j] * (root * root)
            inside = jnp.where(row > j, weight[:8], 0.0)
            weight = jnp.concatenate([inside, weight[8:]], axis=0) if rows > 8 else inside
            for c in range(j + 1, 8):
                columns[c] = columns[c] - weight * columns[c][j : j + 1, :]
            rest = rest - weight * rest[j : j + 1, :]
            carried = carried - weight * carried[j : j + 1, :]
        kept.append(rest[:8] * scale)
        factor.append(carried[:8] * scale)
        rest, carried = rest[8:], carried[8:]
        beside(at // 8)
    return jnp.concatenate(kept, axis=0), jnp.concatenate(factor, axis=0)


def factor_block(rest, carried, beside):
    outs = []
    for first in range(0, LANES, PANEL):
        kept, factor = eliminate(rest[:PANEL], carried[:PANEL], first, beside)
        outs.append(factor)
        if first + PANEL < LANES:
            below = kept.T[first + PANEL :]
            both = jnp.concatenate([kept, factor], axis=1)
            moved = dot(below, both, ((1,), (0,)), EXACT)
            rest, carried = rest[PANEL:] - moved[:, :LANES], carried[PANEL:] - moved[:, LANES:]
    return jnp.concatenate(outs, axis=0)


def whiten_kernel(pixels, place, mine, other, high_hbm, low_hbm, scores_hbm, log_scale, *scratch):
    high, low, out, gram, inverse, both, in_sems, out_sems = scratch
    n = gram.shape[0]
    fetches = [
        pltpu.make_async_copy(high_hbm, high, in_sems.at[0]),
        pltpu.make_async_copy(low_hbm, low, in_sems.at[1]),
    ]
    for fetch in fetches:
        fetch.start()

    def packed(index):
        side, block = divmod(index, 5)
        return jnp.where(place[1] == side, mine[block], other[block])

    shape = (LANES, LANES)
    eye = lax.broadcasted_iota(jnp.int32, shape, 0) == lax.broadcasted_iota(jnp.int32, shape, 1)
    across, down = [], []
    spread = jnp.zeros((1, LANES), jnp.float32)
    for k in range(4):
        index = BLOCKS.index((k, k))
        diagonal = jnp.where(eye, packed(index), 0.0) * (1.0 / pixels)
        flat = jnp.sum(diagonal, axis=0, keepdims=True)
        spread = spread + jnp.where(place[0] == k, flat, 0.0)
        across.append(lax.rsqrt(flat + 1e-05))
        down.append(lax.rsqrt(jnp.sum(diagonal, axis=1, keepdims=True) + 1e-05))
    for index, (i, j) in enumerate(BLOCKS):
        block = packed(index) * (1.0 / pixels) * down[i] * across[j]
        gram[i * LANES : (i + 1) * LANES, j * LANES : (j + 1) * LANES] = block
        if i != j:
            gram[j * LANES : (j + 1) * LANES, i * LANES : (i + 1) * LANES] = block.T

    log_scale[...] = 0.5 * jnp.log(spread + 1e-05)
    plain, lanes = ((1,), (0,)), ((1,), (1,))
    pieces = 16
    rows = high.shape[0] // pieces
    sends = []

    def score(column, piece):
        depth = (column + 1) * LANES
        here = slice(piece * rows, (piece + 1) * rows)
        cols = slice(column * LANES, (column + 1) * LANES)
        wide = dot(high[here, :depth], both[:, :depth], lanes)
        narrow = dot(low[here, :depth], both[:LANES, :depth], lanes)
        out[here, cols] = wide[:, :LANES] + wide[:, LANES:] + narrow
        if piece % 4 == 3:
            done = slice((piece - 3) * rows, (piece + 1) * rows)
            send = pltpu.make_async_copy(
                out.at[done, cols], scores_hbm.at[done, cols], out_sems.at[len(sends)]
            )
            send.start()
            sends.append(send)

    for column in range(4):
        at = column * LANES
        end = at + LANES
        here = slice(at, end)
        if column == 1:
            for fetch in fetches:
                fetch.wait()
        beside = (lambda piece: score(column - 1, piece)) if column else (lambda piece: None)
        own = factor_block(gram[here, here], jnp.where(eye, 1.0, 0.0), beside)
        if at > 0:
            inverse[here, :at] = dot(own, inverse[here, :at], plain, EXACT)
        inverse[here, here] = own
        if end < n:
            right = dot(own, gram[here, end:], plain, EXACT)
            down_side = right.T
            gram[end:, end:] -= dot(down_side, right, plain, EXACT)
            moved = dot(down_side, inverse[here, :end], plain, EXACT)
            if at > 0:
                inverse[end:, :at] -= moved[:, :at]
            inverse[end:, here] = -moved[:, at:]
        scaled = inverse[here, :end] * jnp.concatenate(across[: column + 1], axis=1)
        top = scaled.astype(jnp.bfloat16)
        both[:LANES, :end] = top
        both[LANES:, :end] = (scaled - top.astype(jnp.float32)).astype(jnp.bfloat16)
    for piece in range(pieces):
        score(3, piece)
    for send in sends:
        send.wait()


def whiten(place, mine, other, high, low, pixels):
    rows, n = high.shape
    vmem, hbm = pl.BlockSpec(memory_space=pltpu.VMEM), pl.BlockSpec(memory_space=pl.ANY)
    return pl.pallas_call(
        functools.partial(whiten_kernel, pixels),
        in_specs=[pl.BlockSpec(memory_space=pltpu.SMEM), vmem, vmem, hbm, hbm],
        out_specs=[hbm, vmem],
        out_shape=[
            jax.ShapeDtypeStruct((rows, n), jnp.float32),
            jax.ShapeDtypeStruct((1, LANES), jnp.float32),
        ],
        scratch_shapes=[
            pltpu.VMEM((rows, n), jnp.bfloat16),
            pltpu.VMEM((rows, n), jnp.bfloat16),
            pltpu.VMEM((rows, n), jnp.float32),
            pltpu.VMEM((n, n), jnp.float32),
            pltpu.VMEM((n, n), jnp.float32),
            pltpu.VMEM((2 * LANES, n), jnp.bfloat16),
            pltpu.SemaphoreType.DMA((2,)),
            pltpu.SemaphoreType.DMA((16,)),
        ],
        compiler_params=pltpu.CompilerParams(vmem_limit_bytes=VMEM_LIMIT),
        name="whiten",
    )(place, mine, other, high, low)


def shifted(value, axis, away):
    size = lax.axis_size(axis)
    return lax.ppermute(value, axis, [(k, (k + away) % size) for k in range(size)])


def swapped(value, axis, mask):
    return lax.ppermute(value, axis, [(k, k ^ mask) for k in range(lax.axis_size(axis))])


def summed(mine, other):
    mine = mine + swapped(other, "core", 1)
    share = mine.reshape(16, -1, LANES)
    part = jnp.sum(lax.all_to_all(share, ("x", "z"), 0, 0), axis=0)
    beside, across, askew = (swapped(part, "y", mask) for mask in (1, 2, 3))
    part = (part + beside) + (across + askew)
    spread = jnp.broadcast_to(part, share.shape)
    mine = lax.all_to_all(spread, ("x", "z"), 0, 0).reshape(mine.shape)
    return mine, swapped(mine, "core", 1)


def body(pixel_stack):
    y = lax.axis_index("y")
    lay = lax.axis_size("y")
    pixels = pixel_stack.shape[0] * 32
    blocks = pixel_stack.reshape(lay, -1, LANES)

    def picked(source, chunk, away):
        rows = CHUNKS[chunk]
        start = (lax.rem(y + away, lay), sum(CHUNKS[:chunk]), 0)
        return lax.dynamic_slice(source, start, (1, rows, LANES)).reshape(rows, LANES)

    first = [picked(blocks, 0, away) for away in range(1, lay)]
    stack, _ = lax.optimization_barrier((pixel_stack, first))
    arrived = [[shifted(piece, "y", away) for away, piece in enumerate(first, 1)]]
    total = jnp.sum(stack, axis=0, keepdims=True)
    tail = jnp.broadcast_to(total, (8, LANES))
    pieces = [jnp.concatenate([picked(blocks, 1, away), tail], axis=0) for away in range(1, lay)]
    arrived.append([shifted(piece, "y", away) for away, piece in enumerate(pieces, 1)])
    for chunk in range(2, len(CHUNKS)):
        later, arrived[chunk - 2] = lax.optimization_barrier((blocks, arrived[chunk - 2]))
        arrived.append(
            [shifted(picked(later, chunk, away), "y", away) for away in range(1, lay)]
        )

    sums = jnp.zeros((1, lay * LANES), jnp.float32)
    for away in range(lay):
        value = total if away == 0 else arrived[1][away - 1][-8:-7]
        sums = lax.dynamic_update_slice(sums, value, (0, lax.rem(y - away + lay, lay) * LANES))
    sums = lax.all_to_all(jnp.broadcast_to(sums, (32, 1, lay * LANES)), ("x", "z", "core"), 0, 0)
    means = jnp.sum(sums, axis=0) / pixels

    place = jnp.stack([y, lax.axis_index("core")]).astype(jnp.int32)
    carried = None
    for chunk, pieces in enumerate(arrived):
        carried = gram_chunk(chunk, place, blocks, pieces, means, carried)
    high, low, _, mine, other = carried
    mine, other = summed(mine, other)
    scores, log_scale = whiten(place, mine, other, high, low, pixels)
    return scores, log_scale.reshape(LANES)


def solution(mesh):
    devices = mesh.devices.reshape(4, 4, 2, 4)
    fine = Mesh(devices, ("x", "z", "core", "y"))
    return jax.shard_map(
        body,
        mesh=fine,
        in_specs=(P(("x", "z", "core"), "y"),),
        out_specs=(P(("x", "z", "core", "y"), None), P("y")),
        check_vma=False,
    )
```
